256 devices in a mesh: slab: 64 (over z, y, core), head: 4 (over x).
Axes of the slice: x: 4, y: 4, z: 8, core: 2. Of those that a mesh axis runs over, the one named last changes fastest.
Arguments:
- patches: float32 [16384, 768], P('slab'), may hold values from -6 to 6
- patch_index: int32 [16384], P('slab'), may hold values from 0 to 262143, as said below
- latents: float32 [512, 768], replicated, may hold values from -6 to 6
- w_ref_lat: float32 [768, 768], P(None, 'head')
- w_val_lat: float32 [768, 768], P(None, 'head'), may hold values from -0.21875 to 0.21875
- w_out_lat: float32 [768, 768], P('head'), may hold values from -6 to 6
- w_ref_tok: float32 [768, 768], P(None, 'head')
- w_val_tok: float32 [768, 768], P(None, 'head'), may hold values from -0.21875 to 0.21875
- w_out_tok: float32 [768, 768], P('head'), may hold values from -0.21875 to 0.21875
- grad_tok: float32 [16384, 768], P('slab'), may hold values from -6 to 6
- grad_lat: float32 [512, 768], P(None, 'head'), may hold values from -6 to 6
Outputs:
- latent_out: float32 [512, 768], P(None, 'head')
- token_grad: float32 [16384, 768], P('slab')
- latent_grad: float32 [512, 768], P(None, 'head')
- grad_ref_lat: float32 [768, 768], P(None, 'head')
- grad_val_lat: float32 [768, 768], P(None, 'head')
- grad_out_lat: float32 [768, 768], P('head')
- grad_ref_tok: float32 [768, 768], P(None, 'head')
- grad_val_tok: float32 [768, 768], P(None, 'head')
- grad_out_tok: float32 [768, 768], P('head')
The draws below stay inside these ranges and needn't reach their ends.
Inputs may be any that keep to these rules, and one draw needn't show every extreme that they name: `patch_index`: the 256 indices of one slab device are distinct and lie in its own block of consecutive indices, device k's block starting at k times the block length 64 ** 3 // 64; each block's first and last index appear.
All inputs are finite; a program needn't handle non-finite values.
Results may differ from the reference program's by a relative error of at most 0.0003.
Values sent between devices are 32-bit elements; how exact they have to be, the bound alone decides.
No kernel may reach another device: no remote copies, remote signals or barrier semaphores. Data moves between devices by JAX's collectives and lax.ppermute only.
A program may use at most 192 MiB of HBM per device.

```python
import math
import jax
import jax.numpy as jnp
from jax import lax

D = 768
HEADS = 12
DH = 64
LAT = 512
TOK_DEV = 256
GRID = 64
TOKENS = 16384


def shared_rows(key):
    return jnp.clip(jax.random.normal(key, (TOKENS, D), jnp.float32), -6.0, 6.0)


def draw_patches(key, part):
    row_data = shared_rows(key)
    return row_data


def draw_latents(key, part):
    key = jax.random.fold_in(key, 7)
    latent_rows = jnp.clip(jax.random.normal(key, (LAT, D), jnp.float32), -6.0, 6.0)
    return latent_rows


def draw_w_ref_lat(key, part):
    key = jax.random.fold_in(key, 9)
    return jnp.clip(jax.random.normal(key, (D, D), jnp.float32), -6.0, 6.0) * (2.0 / D) ** 0.5


def draw_w_ref_tok(key, part):
    key = jax.random.fold_in(key, 13)
    fresh = jnp.clip(jax.random.normal(key, (D, D), jnp.float32), -6.0, 6.0) * (2.0 / D) ** 0.5
    return fresh


def draw_patch_index(key, part):
    key = jax.random.fold_in(key, 11)
    devices = TOKENS // TOK_DEV
    block_len = GRID ** 3 // devices

    def one_block(device):
        block_key = jax.random.fold_in(key, device)
        shuffled = jax.random.permutation(block_key, block_len - 2).astype(jnp.int32) + 1
        ends = jnp.array([0, block_len - 1], jnp.int32)
        local = jnp.concatenate([ends, shuffled[:TOK_DEV - 2]])
        return local + device * block_len
    return jax.vmap(one_block)(jnp.arange(devices, dtype=jnp.int32)).reshape(-1).astype(jnp.int32)


def block_levels(own_key, shape, cuts, smallest, high):
    gain = 1.0
    for axis_at, shards_of in cuts:
        steps = jax.random.uniform(jax.random.fold_in(jax.random.fold_in(own_key, 6), axis_at), (shards_of,), jnp.float32, smallest / len(cuts), high / len(cuts))
        gain = gain * jnp.repeat(jnp.exp(steps), shape[axis_at] // shards_of).reshape((-1,) + (1,) * (len(shape) - 1 - axis_at))
    return gain


def noise(stream_key, dims, spread, most, shards=(), kind=jnp.bfloat16):
    gain = block_levels(stream_key, dims, shards, -0.22, 0.18) if shards else 1.0
    drawn = jax.random.normal(stream_key, dims, jnp.float32) * spread * gain
    return jnp.minimum(jnp.maximum(drawn, -most), most).astype(kind)


def setup_inputs(seed: int = 0) -> dict:
    streams_of = jax.random.split(jax.random.key(seed), 12)
    patches = draw_patches(jax.random.fold_in(streams_of[11], 71), 0)
    patch_index = draw_patch_index(jax.random.fold_in(streams_of[11], 71), 0)
    latents = draw_latents(jax.random.fold_in(streams_of[11], 71), 0)
    w_ref_lat = draw_w_ref_lat(jax.random.fold_in(streams_of[11], 71), 0)
    w_val_lat = noise(streams_of[4], (D, D), D ** -0.5, 0.21875, ((1, 4),), jnp.float32)
    w_out_lat = noise(streams_of[5], (D, D), 1.0, 6.0, ((0, 4),), jnp.float32)
    w_ref_tok = draw_w_ref_tok(jax.random.fold_in(streams_of[11], 71), 0)
    w_val_tok = noise(streams_of[7], (D, D), D ** -0.5, 0.21875, ((1, 4),), jnp.float32)
    w_out_tok = noise(streams_of[8], (D, D), D ** -0.5, 0.21875, ((0, 4),), jnp.float32)
    grad_tok = noise(streams_of[9], (TOKENS, D), 1.0, 6.0, ((0, 64),), jnp.float32)
    grad_lat = noise(streams_of[10], (LAT, D), 1.0, 6.0, ((1, 4),), jnp.float32)
    return {"patches": patches, "patch_index": patch_index, "latents": latents, "w_ref_lat": w_ref_lat, "w_val_lat": w_val_lat, "w_out_lat": w_out_lat, "w_ref_tok": w_ref_tok, "w_val_tok": w_val_tok, "w_out_tok": w_out_tok, "grad_tok": grad_tok, "grad_lat": grad_lat}


def position_code(cell_index, width):
    third_width = width // 3
    freq_count = third_width // 2
    coord_a = cell_index // (GRID * GRID)
    coord_b = cell_index // GRID % GRID
    coord_c = cell_index % GRID
    coords = jnp.stack([coord_a, coord_b, coord_c], axis=1).astype(jnp.float32)
    frequency = jnp.exp(jnp.arange(freq_count, dtype=jnp.float32) * (-math.log(10000.0) / freq_count))
    angles = coords[:, :, None] * frequency[None, None, :]
    return jnp.concatenate([jnp.sin(angles), jnp.cos(angles)], axis=2).reshape(cell_index.shape[0], width)

def norm_rows(row_data):
    row_mean = lax.optimization_barrier(jnp.mean(row_data, axis=1, keepdims=True))
    centred = row_data - row_mean
    row_var = lax.optimization_barrier(jnp.mean(centred * centred, axis=1, keepdims=True))
    return centred / jnp.sqrt(row_var + 1e-05)

def product(left_side, right_side):
    return jnp.dot(left_side, right_side, precision=lax.Precision.HIGHEST, preferred_element_type=jnp.float32)

def one_head(pieces):
    latent_keys_proj, latent_value_proj, token_keys_proj, token_value_proj = pieces
    attention_scores = product(latent_keys_proj, token_keys_proj.T) / math.sqrt(DH)
    latent_probabilities = jax.nn.softmax(attention_scores, axis=1)
    token_probabilities = jax.nn.softmax(attention_scores, axis=0)
    return (product(latent_probabilities, token_value_proj), product(token_probabilities.T, latent_value_proj))

def split_by_heads(matrix):
    return matrix.reshape(matrix.shape[0], HEADS, DH).transpose(1, 0, 2)

def joined_heads(stacked):
    return stacked.transpose(1, 0, 2).reshape(stacked.shape[1], D)

def forward(patches, latents, w_ref_lat, w_val_lat, w_out_lat, w_ref_tok, w_val_tok, w_out_tok, code):
    token_normed = norm_rows(patches + code)
    latent_normed = norm_rows(latents)
    pieces = (split_by_heads(product(latent_normed, w_ref_lat)), split_by_heads(product(latent_normed, w_val_lat)), split_by_heads(product(token_normed, w_ref_tok)), split_by_heads(product(token_normed, w_val_tok)))
    lat_attn, token_attention = lax.map(jax.checkpoint(one_head), pieces)
    return (product(joined_heads(lat_attn), w_out_lat), product(joined_heads(token_attention), w_out_tok))

def reference(patches, patch_index, latents, w_ref_lat, w_val_lat, w_out_lat, w_ref_tok, w_val_tok, w_out_tok, grad_tok, grad_lat):
    code = position_code(patch_index, D)

    def apply(*params):
        return forward(*params, code)
    outputs, pullback = jax.vjp(apply, patches, latents, w_ref_lat, w_val_lat, w_out_lat, w_ref_tok, w_val_tok, w_out_tok)
    grads = pullback((grad_lat, grad_tok))
    return (outputs[0], grads[0], grads[1], grads[2], grads[3], grads[4], grads[5], grads[6], grads[7])
```

```python
import functools
import math

import jax
import jax.numpy as jnp
import numpy as np
from jax import lax
from jax.experimental import pallas as pl
from jax.experimental.pallas import tpu as pltpu
from jax.sharding import Mesh, PartitionSpec as P

HEAD = 64
GRID = 64
EPS = 1e-05
F32 = jnp.float32
BF16 = jnp.bfloat16
NN = (((1,), (0,)), ((), ()))
NT = (((1,), (1,)), ((), ()))
SLAB = ("z", "y", "c")
LAT_IN = 5
LAT_OUT = 8
INTERPRET = False


def halves(value):
    high = value.astype(BF16)
    return high, (value - high.astype(F32)).astype(BF16)


def dot3(left, right, dims):
    (lh, ll), (rh, rl) = left, right
    dot = functools.partial(lax.dot_general, dimension_numbers=dims, preferred_element_type=F32)
    return dot(lh, rh) + (dot(lh, rl) + dot(ll, rh))


def pick(pair, rows):
    return pair[0][rows], pair[1][rows]


def call(kernel, outs, name, smem=()):
    def run(*args):
        return pl.pallas_call(
            kernel,
            out_shape=[jax.ShapeDtypeStruct(s, F32) for s in outs],
            in_specs=[
                pl.BlockSpec(memory_space=pltpu.SMEM if i in smem else pltpu.VMEM)
                for i in range(len(args))
            ],
            out_specs=[pl.BlockSpec(memory_space=pltpu.VMEM) for _ in outs],
            compiler_params=pltpu.CompilerParams(vmem_limit_bytes=40 * 1024 * 1024),
            name=name,
            interpret=INTERPRET,
        )(*args)

    return run


def normed(rows):
    centred = rows - jnp.mean(rows, axis=1, keepdims=True)
    inv = 1.0 / jnp.sqrt(jnp.mean(centred * centred, axis=1, keepdims=True) + EPS)
    return centred * inv, inv


def norm_back(upstream, unit, inv):
    return inv * (
        upstream
        - jnp.mean(upstream, axis=1, keepdims=True)
        - unit * jnp.mean(upstream * unit, axis=1, keepdims=True)
    )


def project_kernel(
    patches, code, latents, wrl, wvl, wrt, wvt, tn_o, tinv_o, ln_o, linv_o, q_o, lv_o, k_o, v_o, s_o
):
    tn, tinv = normed(patches[...] + code[...])
    tn_o[...], tinv_o[...] = tn, tinv
    tn = halves(tn)
    k = dot3(halves(wrt[...]), tn, NT)
    k_o[...] = k
    v_o[...] = dot3(halves(wvt[...]), tn, NT)
    ln, linv = normed(latents[...])
    ln_o[...], linv_o[...] = ln, linv
    ln = halves(ln)
    q = dot3(halves(wrl[...]), ln, NT) * (1.0 / math.sqrt(HEAD))
    q_o[...] = q
    lv_o[...] = dot3(halves(wvl[...]), ln, NT)
    q = halves(q)
    for h in range(k.shape[0] // HEAD):
        rows = slice(h * HEAD, (h + 1) * HEAD)
        s_o[h] = dot3(halves(k[rows].T), pick(q, rows), NN)


def latent_kernel(s, v, gl, wol, do_o, dp_o, att_o, st_o):
    heads = s.shape[0]
    do = dot3(halves(wol[...]), halves(gl[...]), NN)
    do_o[...] = do
    do = halves(do)
    st_o[...] = jnp.zeros_like(st_o)
    for h in range(heads):
        rows = slice(h * HEAD, (h + 1) * HEAD)
        sh = s[h]
        top = jnp.max(sh, axis=0, keepdims=True)
        e = jnp.exp(sh - top)
        vh = v[rows, :]
        dp = dot3(halves(vh.T), pick(do, rows), NN)
        dp_o[h] = dp
        st_o[h : h + 1, :] = top
        st_o[heads + h : heads + h + 1, :] = jnp.sum(e, axis=0, keepdims=True)
        st_o[2 * heads + h : 2 * heads + h + 1, :] = jnp.sum(e * dp, axis=0, keepdims=True)
        att_o[rows, :] = dot3(halves(vh), halves(e), NN)


def token_kernel(s, lv, gt, wot, ds_o, dvl_o, got_o):
    gts = halves(gt[...])
    do = dot3(halves(wot[...]), gts, NT)
    lvs = halves(lv[...])
    att = []
    for h in range(s.shape[0]):
        rows = slice(h * HEAD, (h + 1) * HEAD)
        sh = s[h]
        e = jnp.exp(sh - jnp.max(sh, axis=1, keepdims=True))
        p = e * (1.0 / jnp.sum(e, axis=1, keepdims=True))
        ps = halves(p)
        lvh = pick(lvs, rows)
        att.append(dot3(lvh, ps, NT))
        doh = do[rows]
        dp = dot3(halves(doh.T), lvh, NN)
        ds_o[h] = p * (dp - jnp.sum(p * dp, axis=1, keepdims=True))
        dvl_o[rows, :] = dot3(halves(doh), ps, NN)
    got_o[...] = dot3(halves(jnp.concatenate(att, axis=0)), gts, NN)


def backward_kernel(
    s, dp, dst, local, whole, q, k, do, att, tn, wrt, wvt, dvl, got, dtn_o, pack_o
):
    heads = s.shape[0]
    chunks, slots = pack_o.shape[:2]
    wslots = slots - LAT_IN
    qs, ks, dos = halves(q[...]), halves(k[...]), halves(do[...])
    drt, dvt, drl, lat = [], [], [], []
    for h in range(heads):
        rows = slice(h * HEAD, (h + 1) * HEAD)
        top = whole[h : h + 1, :]
        inv = 1.0 / whole[heads + h : heads + h + 1, :]
        delta = whole[2 * heads + h : 2 * heads + h + 1, :] * inv
        p = jnp.exp(s[h] - top) * inv
        ds = halves(p * (dp[h] - delta) + dst[h])
        drt.append(dot3(pick(qs, rows), ds, NT))
        dvt.append(dot3(pick(dos, rows), halves(p), NT))
        drl.append(dot3(pick(ks, rows), ds, NN) * (1.0 / math.sqrt(HEAD)))
        lat.append(att[rows, :] * (jnp.exp(local[h : h + 1, :] - top) * inv))
    both = jnp.concatenate(drt + dvt, axis=0)
    w = halves(jnp.concatenate([wrt[...], wvt[...]], axis=0))
    dtn_o[...] = dot3(halves(both.T), w, NN)
    grads = dot3(halves(both), halves(tn[...]), NN)
    width = drl[0].shape[1]
    rows = jnp.concatenate(
        drl + [dvl[...]] + lat + [jnp.zeros((HEAD, width), F32)], axis=0
    )
    for t in range(LAT_IN):
        pack_o[:, wslots + t] = rows[t * 128 : (t + 1) * 128].T.reshape(chunks, 8, 128)
    index = 0
    for part in (grads, got[...]):
        for r in range(part.shape[0] // 8):
            for l in range(part.shape[1] // 128):
                pack_o[index // wslots, index % wslots] = part[
                    r * 8 : (r + 1) * 8, l * 128 : (l + 1) * 128
                ]
                index += 1
    for index in range(index, chunks * wslots):
        pack_o[index // wslots, index % wslots] = jnp.zeros((8, 128), F32)


def rows_kernel(chunk, wrl, wvl, wol, out):
    wslots = chunk.shape[1] - LAT_IN
    width = wrl.shape[0]
    lat = jnp.concatenate([chunk[0, wslots + t] for t in range(LAT_IN)], axis=1)
    lat = halves(lat)
    cols = [(p[:, i * width : (i + 1) * width]) for i in range(3) for p in lat]
    dref, dval, att = cols[0:2], cols[2:4], cols[4:6]
    out[:, : wrl.shape[1]] = dot3(dref, halves(wrl[...]), NN) + dot3(dval, halves(wvl[...]), NN)
    out[:, wrl.shape[1] :] = dot3(att, halves(wol[...]), NN)


def finish_kernel(chunk, ln, linv, share, *refs):
    parts, out = refs[:-1], refs[-1]
    wslots = chunk.shape[1] - LAT_IN
    total = parts[0][...]
    for p in parts[1:]:
        total = total + p[...]
    full = total.shape[1] // 2
    width = full // len(parts)
    grad = norm_back(total[:, :full], ln[...], linv[...])
    own_grad = jnp.zeros((8, width), F32)
    own_out = jnp.zeros((8, width), F32)
    for i in range(len(parts)):
        here = share[0] == i
        own_grad = jnp.where(here, grad[:, i * width : (i + 1) * width], own_grad)
        at = full + i * width
        own_out = jnp.where(here, total[:, at : at + width], own_out)
    lat = jnp.concatenate([chunk[0, wslots + t] for t in range(LAT_IN)], axis=1)
    lat = jnp.concatenate(
        [lat[:, : 3 * width], own_grad, own_out, jnp.zeros((8, LAT_OUT * 128 - 5 * width), F32)],
        axis=1,
    )
    for t in range(wslots):
        out[0, t] = chunk[0, t]
    for t in range(LAT_OUT):
        out[0, wslots + t] = lat[:, t * 128 : (t + 1) * 128]


def unpack_kernel(pack, ln, gl, grl_o, gvl_o, gol_o, grt_o, gvt_o, got_o, lg_o, lo_o):
    chunks, slots = pack.shape[:2]
    wslots = slots - LAT_OUT
    width = grl_o.shape[0]
    rows = jnp.concatenate(
        [pack[:, wslots + t].reshape(chunks * 8, 128).T for t in range(LAT_OUT)], axis=0
    )
    lns = halves(ln[...])
    grl_o[...] = dot3(halves(rows[:width]), lns, NN)
    gvl_o[...] = dot3(halves(rows[width : 2 * width]), lns, NN)
    gol_o[...] = dot3(halves(rows[2 * width : 3 * width]), halves(gl[...]), NT)
    lg_o[...] = rows[3 * width : 4 * width]
    lo_o[...] = rows[4 * width : 5 * width]
    index = 0
    for part in (grt_o, gvt_o, got_o):
        for r in range(part.shape[0] // 8):
            for l in range(part.shape[1] // 128):
                part[r * 8 : (r + 1) * 8, l * 128 : (l + 1) * 128] = pack[
                    index // wslots, index % wslots
                ]
                index += 1


def position_code(cell_index, width):
    third = width // 3
    count = third // 2
    coords = jnp.stack(
        [cell_index // (GRID * GRID), cell_index // GRID % GRID, cell_index % GRID], axis=1
    ).astype(F32)
    frequency = jnp.exp(jnp.arange(count, dtype=F32) * (-math.log(10000.0) / count))
    angles = coords[:, :, None] * frequency[None, None, :]
    return jnp.concatenate([jnp.sin(angles), jnp.cos(angles)], axis=2).reshape(
        cell_index.shape[0], width
    )


def shift(value, axis, by):
    n = lax.axis_size(axis)
    return lax.ppermute(value, axis, [(i, (i + by) % n) for i in range(n)])


def scatter_sum(value, axis):
    n, me = lax.axis_size(axis), lax.axis_index(axis)
    size = value.shape[0] // n
    block = lambda j: lax.dynamic_slice_in_dim(value, (j % n) * size, size, 0)
    got = [shift(block(me + by), axis, by) for by in range(1, n)]
    total = block(me)
    for g in got:
        total = total + g
    return total


def gather(value, axis):
    n, me = lax.axis_size(axis), lax.axis_index(axis)
    size = value.shape[0]
    got = [shift(value, axis, by) for by in range(1, n)]
    whole = jnp.zeros((n * size,) + value.shape[1:], value.dtype)
    whole = lax.dynamic_update_slice_in_dim(whole, value, me * size, 0)
    for by, g in zip(range(1, n), got):
        whole = lax.dynamic_update_slice_in_dim(whole, g, ((me - by) % n) * size, 0)
    return whole


def merge_stats(stats, heads, axis):
    n = lax.axis_size(axis)
    all_stats = [stats] + [shift(stats, axis, by) for by in range(1, n)]
    top = functools.reduce(jnp.maximum, [a[:heads] for a in all_stats])
    total = sums = 0.0
    for a in all_stats:
        scale = jnp.exp(a[:heads] - top)
        total = total + a[heads : 2 * heads] * scale
        sums = sums + a[2 * heads : 3 * heads] * scale
    pad = jnp.zeros((stats.shape[0] - 3 * heads, stats.shape[1]), F32)
    return jnp.concatenate([top, total, sums, pad], axis=0)


def body(
    patches,
    patch_index,
    latents,
    w_ref_lat,
    w_val_lat,
    w_out_lat,
    w_ref_tok,
    w_val_tok,
    w_out_tok,
    grad_tok,
    grad_lat,
):
    tokens, full = patches.shape
    lats = latents.shape[0]
    width = w_ref_lat.shape[1]
    heads = width // HEAD
    chunks = math.prod(lax.axis_size(a) for a in SLAB)
    assert lats == 8 * chunks
    wslots = -(-3 * (width // 8) * (full // 128) // chunks)
    wrl, wvl, wrt, wvt = w_ref_lat.T, w_val_lat.T, w_ref_tok.T, w_val_tok.T
    core = lax.axis_index("c")

    cores = lax.axis_size("c")
    part = lax.dynamic_slice_in_dim(grad_lat.T, core * (width // cores), width // cores, 0)
    mine = gather(part[None], "x")
    other = shift(mine, "c", 1)
    pair = jnp.where(
        core == 0, jnp.stack([mine, other], axis=1), jnp.stack([other, mine], axis=1)
    )
    gl = pair.reshape(full, lats)

    square = (heads, tokens, lats)
    tn, tinv, ln, linv, q, lv, k, v, s = call(
        project_kernel,
        [
            (tokens, full),
            (tokens, 1),
            (lats, full),
            (lats, 1),
            (width, lats),
            (width, lats),
            (width, tokens),
            (width, tokens),
            square,
        ],
        "project",
    )(patches, position_code(patch_index, full), latents, wrl, wvl, wrt, wvt)
    do, dp, att, local = call(
        latent_kernel, [(width, lats), square, (width, lats), (16, lats)], "latent"
    )(s, v, gl, w_out_lat)
    whole = local
    for axis in ("c", "y", "z"):
        whole = merge_stats(whole, heads, axis)
    dst, dvl, got = call(token_kernel, [square, (width, lats), (width, full)], "token")(
        s, lv, grad_tok, w_out_tok
    )
    dtn, pack = call(
        backward_kernel, [(tokens, full), (chunks, wslots + LAT_IN, 8, 128)], "backward"
    )(s, dp, dst, local, whole, q, k, do, att, tn, wrt, wvt, dvl, got)

    share = lax.axis_index("x")
    rows = tokens // lax.axis_size("x")
    own = scatter_sum(dtn, "x")
    own = norm_back(
        own,
        lax.dynamic_slice_in_dim(tn, share * rows, rows, 0),
        lax.dynamic_slice_in_dim(tinv, share * rows, rows, 0),
    )
    token_grad = gather(own, "x")

    chunk = scatter_sum(scatter_sum(scatter_sum(pack, "c"), "y"), "z")
    (part,) = call(rows_kernel, [(8, 2 * full)], "rows")(chunk, wrl, wvl, w_out_lat)
    others = [shift(part, "x", by) for by in range(1, lax.axis_size("x"))]
    at = 0
    for axis in ("c", "y", "z"):
        at = at * lax.axis_size(axis) + lax.axis_index(axis)
    (chunk,) = call(finish_kernel, [(1, wslots + LAT_OUT, 8, 128)], "finish", smem=(3,))(
        chunk,
        lax.dynamic_slice_in_dim(ln, at * 8, 8, 0),
        lax.dynamic_slice_in_dim(linv, at * 8, 8, 0),
        share.reshape(1),
        part,
        *others,
    )
    pack = gather(gather(gather(chunk, "z"), "y"), "c")
    grl, gvl, gol, grt, gvt, got, lg, lo = call(
        unpack_kernel, [(width, full)] * 6 + [(width, lats)] * 2, "unpack"
    )(pack, ln, gl)
    return lo.T, token_grad, lg.T, grl.T, gvl.T, gol, grt.T, gvt.T, got


def solution(mesh):
    sizes = mesh.devices.shape
    split = {64: (8, 4, 2), 8: (2, 2, 2)}[sizes[0]]
    fine = Mesh(mesh.devices.reshape(*split, sizes[1]), (*SLAB, "x"))
    rows, cols, lead = P(SLAB, None), P(None, "x"), P("x", None)
    in_specs = (rows, P(SLAB), P(), cols, cols, lead, cols, cols, lead, rows, cols)
    out_specs = (cols, rows, cols, cols, cols, lead, cols, cols, lead)
    return jax.shard_map(
        body, mesh=fine, in_specs=in_specs, out_specs=out_specs, check_vma=False
    )
```

```python
import functools
import math

import jax
import jax.numpy as jnp
from jax import lax
from jax.experimental import pallas as pl
from jax.experimental.pallas import tpu as pltpu
from jax.sharding import Mesh, PartitionSpec as P

HEAD = 64
GRID = 64
EPS = 1e-05
F32 = jnp.float32
BF16 = jnp.bfloat16
NN = (((1,), (0,)), ((), ()))
NT = (((1,), (1,)), ((), ()))
SLAB = ("u", "w", "y", "c")
LAT_IN = 5
LAT_OUT = 8
INTERPRET = False
VMEM_BYTES = 24 * 1024 * 1024


def halves(value):
    high = value.astype(BF16)
    return high, (value - high.astype(F32)).astype(BF16)


def dot3(left, right, dims):
    (lh, ll), (rh, rl) = left, right
    dot = functools.partial(lax.dot_general, dimension_numbers=dims, preferred_element_type=F32)
    return dot(lh, rh) + (dot(lh, rl) + dot(ll, rh))


def pick(pair, rows):
    return pair[0][rows], pair[1][rows]


def call(kernel, outs, name, scratch=(), smem=(), flops=0):
    def run(*args):
        moved = sum(math.prod(a.shape) for a in args) + sum(math.prod(o) for o in outs)
        return pl.pallas_call(
            kernel,
            out_shape=[jax.ShapeDtypeStruct(o, F32) for o in outs],
            in_specs=[
                pl.BlockSpec(memory_space=pltpu.SMEM if i in smem else pltpu.VMEM)
                for i in range(len(args))
            ],
            out_specs=[pl.BlockSpec(memory_space=pltpu.VMEM) for _ in outs],
            scratch_shapes=[pltpu.VMEM(shape, F32) for shape in scratch],
            compiler_params=pltpu.CompilerParams(vmem_limit_bytes=VMEM_BYTES),
            cost_estimate=pl.CostEstimate(
                flops=flops, bytes_accessed=4 * moved, transcendentals=0
            ),
            name=name,
            interpret=INTERPRET,
        )(*args)

    return run


def normed(rows):
    centred = rows - jnp.mean(rows, axis=1, keepdims=True)
    inv = 1.0 / jnp.sqrt(jnp.mean(centred * centred, axis=1, keepdims=True) + EPS)
    return centred * inv, inv


def norm_back(upstream, unit, inv):
    return inv * (
        upstream
        - jnp.mean(upstream, axis=1, keepdims=True)
        - unit * jnp.mean(upstream * unit, axis=1, keepdims=True)
    )


def project_kernel(
    patches, latents, wrl, wvl, wrt, wvt, cells, table, place,
    tn_o, tno_o, tio_o, ln_o, lno_o, lio_o, q_o, lv_o, k_o, v_o, s_o,
    tinv_s, linv_s,
):
    cell = cells[...]
    terms = []
    rest = table[...]
    for _ in range(3):
        terms.append(rest.astype(BF16))
        rest = rest - terms[-1].astype(F32)
    code = []
    for coord in (cell // (GRID * GRID), cell // GRID % GRID, cell % GRID):
        hot = lax.broadcasted_iota(jnp.int32, (GRID, cell.shape[1]), 0) == coord
        hot = jnp.where(hot, 1.0, 0.0).astype(F32).T.astype(BF16)
        dot = functools.partial(
            lax.dot_general, hot, dimension_numbers=NN, preferred_element_type=F32
        )
        code.append(dot(terms[0]) + (dot(terms[1]) + dot(terms[2])))
    tn, tinv_s[...] = normed(patches[...] + jnp.concatenate(code, axis=1))
    tn_o[...] = tn
    rows = tno_o.shape[0]
    mine = pl.ds(pl.multiple_of(place[4] * rows, 8), rows)
    tno_o[...] = tn_o[mine, :]
    tio_o[...] = tinv_s[mine, :]
    tn = halves(tn)
    k = dot3(halves(wrt[...]), tn, NT)
    k_o[...] = k
    v_o[...] = dot3(halves(wvt[...]), tn, NT)
    ln, linv_s[...] = normed(latents[...])
    ln_o[...] = ln
    mine = pl.ds(pl.multiple_of(place[5] * 8, 8), 8)
    lno_o[...] = ln_o[mine, :]
    lio_o[...] = linv_s[mine, :]
    ln = halves(ln)
    q = dot3(halves(wrl[...]), ln, NT) * (1.0 / math.sqrt(HEAD))
    q_o[...] = q
    lv_o[...] = dot3(halves(wvl[...]), ln, NT)
    q = halves(q)
    for h in range(k.shape[0] // HEAD):
        rows = slice(h * HEAD, (h + 1) * HEAD)
        s_o[h] = dot3(halves(k[rows].T), pick(q, rows), NN)


def latent_kernel(place, s, v, wol, *refs):
    pieces, (gl_o, do_o, dp_o, att_o, st_o) = refs[:-5], refs[-5:]
    shares = len(pieces) // 2
    size = pieces[0].shape[0]
    for j in range(2):
        for d in range(shares):
            share = (place[4] + shares - d) % shares
            at = share * (2 * size) + (place[3] ^ j) * size
            gl_o[pl.ds(pl.multiple_of(at, 8), size), :] = pieces[j * shares + d][...]
    heads = s.shape[0]
    do = dot3(halves(wol[...]), halves(gl_o[...]), NN)
    do_o[...] = do
    do = halves(do)
    st_o[...] = jnp.zeros_like(st_o)
    for h in range(heads):
        rows = slice(h * HEAD, (h + 1) * HEAD)
        sh = s[h]
        top = jnp.max(sh, axis=0, keepdims=True)
        e = jnp.exp(sh - top)
        vh = v[rows, :]
        dp = dot3(halves(vh.T), pick(do, rows), NN)
        dp_o[h] = dp
        st_o[h : h + 1, :] = top
        st_o[heads + h : heads + h + 1, :] = jnp.sum(e, axis=0, keepdims=True)
        st_o[2 * heads + h : 2 * heads + h + 1, :] = jnp.sum(e * dp, axis=0, keepdims=True)
        att_o[rows, :] = dot3(halves(vh), halves(e), NN)


def merge_kernel(heads, *refs):
    parts, out = refs[:-1], refs[-1]
    top = functools.reduce(jnp.maximum, [p[:heads, :] for p in parts])
    total = sums = 0.0
    for p in parts:
        scale = jnp.exp(p[:heads, :] - top)
        total = total + p[heads : 2 * heads, :] * scale
        sums = sums + p[2 * heads : 3 * heads, :] * scale
    pad = jnp.zeros((out.shape[0] - 3 * heads, out.shape[1]), F32)
    out[...] = jnp.concatenate([top, total, sums, pad], axis=0)


def token_kernel(s, lv, gt, wot, ds_o, dvl_o, got_o):
    gts = halves(gt[...])
    do = dot3(halves(wot[...]), gts, NT)
    lvs = halves(lv[...])
    att = []
    for h in range(s.shape[0]):
        rows = slice(h * HEAD, (h + 1) * HEAD)
        sh = s[h]
        e = jnp.exp(sh - jnp.max(sh, axis=1, keepdims=True))
        p = e * (1.0 / jnp.sum(e, axis=1, keepdims=True))
        ps = halves(p)
        lvh = pick(lvs, rows)
        att.append(dot3(lvh, ps, NT))
        doh = do[rows]
        dp = dot3(halves(doh.T), lvh, NN)
        ds_o[h] = p * (dp - jnp.sum(p * dp, axis=1, keepdims=True))
        dvl_o[rows, :] = dot3(halves(doh), ps, NN)
    got_o[...] = dot3(halves(jnp.concatenate(att, axis=0)), gts, NN)


SEND_KEEP = (((1, 2), (0, 3)), ((3, 2), (0, 1)))


def backward_kernel(
    place, s, dp, dst, local, whole, q, k, do, att, tn, wrt, wvt, dvl, got, *refs
):
    outs, (dtn_s, pack_s) = refs[:-2], refs[-2:]
    dtn_o, pack_o = outs[:-8], outs[-8:]
    heads = s.shape[0]
    chunks, slots = pack_s.shape[:2]
    wslots = slots - LAT_IN
    qs, ks, dos = halves(q[...]), halves(k[...]), halves(do[...])
    drt, dvt, drl, lat = [], [], [], []
    for h in range(heads):
        rows = slice(h * HEAD, (h + 1) * HEAD)
        top = whole[h : h + 1, :]
        inv = 1.0 / whole[heads + h : heads + h + 1, :]
        delta = whole[2 * heads + h : 2 * heads + h + 1, :] * inv
        p = jnp.exp(s[h] - top) * inv
        ds = halves(p * (dp[h] - delta) + dst[h])
        drt.append(dot3(pick(qs, rows), ds, NT))
        dvt.append(dot3(pick(dos, rows), halves(p), NT))
        drl.append(dot3(pick(ks, rows), ds, NN) * (1.0 / math.sqrt(HEAD)))
        lat.append(att[rows, :] * (jnp.exp(local[h : h + 1, :] - top) * inv))
    width = drl[0].shape[1]
    rows = jnp.concatenate(
        drl + [dvl[...]] + lat + [jnp.zeros((HEAD, width), F32)], axis=0
    )
    for t in range(LAT_IN):
        pack_s[:, wslots + t] = rows[t * 128 : (t + 1) * 128].T.reshape(chunks, 8, 128)
    both = jnp.concatenate(drt + dvt, axis=0)
    grads = dot3(halves(both), halves(tn[...]), NN)
    index = 0
    for part in (grads, got[...]):
        for r in range(part.shape[0] // 8):
            for l in range(part.shape[1] // 128):
                pack_s[index // wslots, index % wslots] = part[
                    r * 8 : (r + 1) * 8, l * 128 : (l + 1) * 128
                ]
                index += 1
    for index in range(index, chunks * wslots):
        pack_s[index // wslots, index % wslots] = jnp.zeros((8, 128), F32)
    us = pack_o[0].shape[1]
    for j in range(2):
        for half in range(2):
            for kind in range(2):
                out = pack_o[j * 4 + half * 2 + kind]
                for i, flip in enumerate(SEND_KEEP[half][kind]):
                    for d in range(us):
                        u = (place[0] + d) % us
                        out[i, d] = pack_s[
                            chunk_at(u, place[1] ^ half, place[2] ^ flip, place[3] ^ j)
                        ]
    w = halves(jnp.concatenate([wrt[...], wvt[...]], axis=0))
    dtn_s[...] = dot3(halves(both.T), w, NN)
    size = dtn_o[0].shape[0]
    for d, out in enumerate(dtn_o):
        at = (place[4] + d) % len(dtn_o) * size
        out[...] = dtn_s[pl.ds(pl.multiple_of(at, 8), size), :]


def chunk_at(u, w, y, c):
    return ((u * 2 + w) * 4 + y) * 2 + c


def own_rows_kernel(unit, inv, *refs):
    total = refs[0][...]
    for p in refs[1:-1]:
        total = total + p[...]
    refs[-1][...] = norm_back(total, unit[...], inv[...])


def join_rows_kernel(place, *refs):
    parts, out = refs[:-1], refs[-1]
    size = parts[0].shape[0]
    for d, p in enumerate(parts):
        at = (place[4] + len(parts) - d) % len(parts) * size
        out[pl.ds(pl.multiple_of(at, 8), size), :] = p[...]


def join_kernel(*refs):
    for i, p in enumerate(refs[:-1]):
        refs[-1][i] = p[0]


def rows_kernel(wrl, wvl, wol, *refs):
    parts, (chunk, out) = refs[:-2], refs[-2:]
    total = parts[0][0]
    for p in parts[1:]:
        total = total + p[0]
    chunk[0] = total
    wslots = chunk.shape[1] - LAT_IN
    width, full = wrl.shape
    lat = halves(jnp.concatenate([total[wslots + t] for t in range(LAT_IN)], axis=1))
    dref, dval, att = [
        tuple(p[:, i * width : (i + 1) * width] for p in lat) for i in range(3)
    ]
    out[:, :full] = dot3(dref, halves(wrl[...]), NN) + dot3(dval, halves(wvl[...]), NN)
    out[:, full:] = dot3(att, halves(wol[...]), NN)


def finish_kernel(place, chunk, ln, linv, *refs):
    parts, out = refs[:-1], refs[-1]
    wslots = chunk.shape[1] - LAT_IN
    total = parts[0][...]
    for p in parts[1:]:
        total = total + p[...]
    full = total.shape[1] // 2
    width = full // len(parts)
    grad = norm_back(total[:, :full], ln[...], linv[...])
    own_grad = jnp.zeros((8, width), F32)
    own_out = jnp.zeros((8, width), F32)
    for i in range(len(parts)):
        here = place[4] == i
        own_grad = jnp.where(here, grad[:, i * width : (i + 1) * width], own_grad)
        at = full + i * width
        own_out = jnp.where(here, total[:, at : at + width], own_out)
    lat = jnp.concatenate([chunk[0, wslots + t] for t in range(LAT_IN)], axis=1)
    lat = jnp.concatenate(
        [lat[:, : 3 * width], own_grad, own_out, jnp.zeros((8, LAT_OUT * 128 - 5 * width), F32)],
        axis=1,
    )
    for t in range(wslots):
        out[0, t] = chunk[0, t]
    for t in range(LAT_OUT):
        out[0, wslots + t] = lat[:, t * 128 : (t + 1) * 128]


def unpack_kernel(place, ln, gl, *refs):
    parts, outs, pack = refs[:16], refs[16:-1], refs[-1]
    grl_o, gvl_o, gol_o, grt_o, gvt_o, got_o, lg_o, lo_o = outs
    us = parts[0].shape[0]
    for j in range(2):
        for half in range(2):
            for flip in range(4):
                part = parts[j * 8 + half * 4 + flip]
                for d in range(us):
                    u = (place[0] + us - d) % us
                    pack[chunk_at(u, place[1] ^ half, place[2] ^ flip, place[3] ^ j)] = part[d]
    chunks, slots = pack.shape[:2]
    wslots = slots - LAT_OUT
    width = grl_o.shape[0]
    rows = jnp.concatenate(
        [pack[:, wslots + t].reshape(chunks * 8, 128).T for t in range(LAT_OUT)], axis=0
    )
    lns = halves(ln[...])
    grl_o[...] = dot3(halves(rows[:width]), lns, NN)
    gvl_o[...] = dot3(halves(rows[width : 2 * width]), lns, NN)
    gol_o[...] = dot3(halves(rows[2 * width : 3 * width]), halves(gl[...]), NT)
    lg_o[...] = rows[3 * width : 4 * width]
    lo_o[...] = rows[4 * width : 5 * width]
    index = 0
    for part in (grt_o, gvt_o, got_o):
        for r in range(part.shape[0] // 8):
            for l in range(part.shape[1] // 128):
                part[r * 8 : (r + 1) * 8, l * 128 : (l + 1) * 128] = pack[
                    index // wslots, index % wslots
                ]
                index += 1


def code_table(width):
    count = width // 6
    frequency = jnp.exp(jnp.arange(count, dtype=F32) * (-math.log(10000.0) / count))
    angles = jnp.arange(GRID, dtype=F32)[:, None] * frequency[None, :]
    return jnp.concatenate([jnp.sin(angles), jnp.cos(angles)], axis=1)


def shift(value, axis, by):
    n = lax.axis_size(axis)
    return lax.ppermute(value, axis, [(i, (i + by) % n) for i in range(n)])


def shifts(value, axis):
    return [shift(value, axis, by) for by in range(1, lax.axis_size(axis))]


def swap(value, axis, flip=1):
    return lax.ppermute(value, axis, [(i, i ^ flip) for i in range(lax.axis_size(axis))])


def body(
    patches,
    patch_index,
    latents,
    w_ref_lat,
    w_val_lat,
    w_out_lat,
    w_ref_tok,
    w_val_tok,
    w_out_tok,
    grad_tok,
    grad_lat,
):
    tokens, full = patches.shape
    lats = latents.shape[0]
    width = w_ref_lat.shape[1]
    heads = width // HEAD
    u, w, y, c, x = (lax.axis_index(a) for a in (*SLAB, "x"))
    us, xs = lax.axis_size("u"), lax.axis_size("x")
    chunks = us * 16
    assert lats == 8 * chunks
    wslots = -(-3 * (width // 8) * (full // 128) // chunks)
    wrl, wvl, wrt, wvt = w_ref_lat.T, w_val_lat.T, w_ref_tok.T, w_val_tok.T
    place = jnp.stack([u, w, y, c, x, chunk_at(u, w, y, c)]).astype(jnp.int32)

    half = width // 2
    part = lax.dynamic_slice_in_dim(grad_lat.T, c * half, half, 0)
    mine = shifts(part, "x")

    square = (heads, tokens, lats)
    rows = tokens // xs
    tn, tn_own, tinv, ln, ln_own, linv, q, lv, k, v, s = call(
        project_kernel,
        [
            (tokens, full),
            (rows, full),
            (rows, 1),
            (lats, full),
            (8, full),
            (8, 1),
            (width, lats),
            (width, lats),
            (width, tokens),
            (width, tokens),
            square,
        ],
        "project",
        scratch=[(tokens, 1), (lats, 1)],
        smem=(8,),
        flops=6 * width * full * (2 * tokens + 2 * lats),
    )(
        patches,
        latents,
        wrl,
        wvl,
        wrt,
        wvt,
        patch_index.reshape(1, tokens),
        code_table(full),
        place,
    )
    *mine, s = lax.optimization_barrier((*mine, s))
    mine = [part] + mine
    pieces = mine + [swap(p, "c") for p in mine]
    gl, do, dp, att, local = call(
        latent_kernel,
        [(full, lats), (width, lats), square, (width, lats), (16, lats)],
        "latent",
        smem=(0,),
        flops=6 * width * lats * (full + 2 * tokens),
    )(place, s, v, w_out_lat, *pieces)

    def merge(parts):
        return call(functools.partial(merge_kernel, heads), [(16, lats)], "merge")(*parts)[0]

    whole = merge([local, swap(local, "c")])
    whole = merge([whole] + shifts(whole, "y"))
    whole = merge([whole, swap(whole, "w")])
    whole = merge([whole] + shifts(whole, "u"))
    dst, dvl, got = call(
        token_kernel,
        [square, (width, lats), (width, full)],
        "token",
        flops=6 * width * tokens * (2 * full + 3 * lats),
    )(s, lv, grad_tok, w_out_tok)
    outs = call(
        backward_kernel,
        [(rows, full)] * xs + [(2, us, wslots + LAT_IN, 8, 128)] * 8,
        "backward",
        scratch=[(tokens, full), (chunks, wslots + LAT_IN, 8, 128)],
        smem=(0,),
        flops=6 * width * tokens * (4 * full + 3 * lats),
    )(place, s, dp, dst, local, whole, q, k, do, att, tn, wrt, wvt, dvl, got)
    dtn, packs = outs[:xs], outs[xs:]

    moved = [swap(p, "c") for p in (packs[4], packs[6], packs[5], packs[7])]
    send_a, send_b, keep_a, keep_b = [
        a + b for a, b in zip((packs[0], packs[2], packs[1], packs[3]), moved)
    ]
    got_a, got_b = swap(send_a, "y", 1), swap(send_b, "y", 3)
    own = [dtn[0]] + [shift(d, "x", by) for by, d in enumerate(dtn[1:], 1)]
    keep_a, keep_b = keep_a + got_a, keep_b + got_b
    sum_a = keep_a[0] + swap(keep_a[1], "y", 3)
    sum_b = keep_b[0] + swap(keep_b[1], "y", 1)
    *own, sum_b = lax.optimization_barrier((*own, sum_b))
    (own,) = call(own_rows_kernel, [(rows, full)], "own_rows")(tn_own, tinv, *own)
    owns = [own] + shifts(own, "x")
    sums = sum_a + swap(sum_b, "w")
    blocks = [sums[:1]] + [shift(sums[d : d + 1], "u", d) for d in range(1, us)]
    *owns, blocks[-1] = lax.optimization_barrier((*owns, blocks[-1]))
    chunk, part = call(
        rows_kernel, [(1, wslots + LAT_IN, 8, 128), (8, 2 * full)], "rows"
    )(wrl, wvl, w_out_lat, *blocks)
    (chunk,) = call(finish_kernel, [(1, wslots + LAT_OUT, 8, 128)], "finish", smem=(0,))(
        place, chunk, ln_own, linv, part, *shifts(part, "x")
    )
    (four,) = call(join_kernel, [(us, wslots + LAT_OUT, 8, 128)], "join")(
        chunk, *shifts(chunk, "u")
    )
    other = swap(four, "w")
    a1, a3, b1, b3 = swap(four, "y", 1), swap(four, "y", 3), swap(other, "y", 1), swap(other, "y", 3)
    (token_grad,) = call(join_rows_kernel, [(tokens, full)], "join_rows", smem=(0,))(
        place, *owns
    )
    parts = [four, a1, swap(a3, "y", 1), a3, other, b1, swap(b1, "y", 3), b3]
    parts += [swap(p, "c") for p in parts]
    grl, gvl, gol, grt, gvt, got, lg, lo = call(
        unpack_kernel,
        [(width, full)] * 6 + [(width, lats)] * 2,
        "unpack",
        scratch=[(chunks, wslots + LAT_OUT, 8, 128)],
        smem=(0,),
        flops=18 * width * lats * full,
    )(place, ln, gl, *parts)
    return lo.T, token_grad, lg.T, grl.T, gvl.T, gol, grt.T, gvt.T, got


def solution(mesh):
    slab, head = mesh.devices.shape
    fine = Mesh(mesh.devices.reshape(slab // 16, 2, 4, 2, head), (*SLAB, "x"))
    rows, cols, lead = P(SLAB, None), P(None, "x"), P("x", None)
    in_specs = (rows, P(SLAB), P(), cols, cols, lead, cols, cols, lead, rows, cols)
    out_specs = (cols, rows, cols, cols, cols, lead, cols, cols, lead)
    return jax.shard_map(
        body, mesh=fine, in_specs=in_specs, out_specs=out_specs, check_vma=False
    )
```

```python
import functools
import math

import jax
import jax.numpy as jnp
from jax import lax
from jax.experimental import pallas as pl
from jax.experimental.pallas import tpu as pltpu
from jax.sharding import Mesh, PartitionSpec as P

HEAD = 64
GRID = 64
EPS = 1e-05
F32 = jnp.float32
BF16 = jnp.bfloat16
NN = (((1,), (0,)), ((), ()))
NT = (((1,), (1,)), ((), ()))
SLAB = ("u", "w", "y", "c")
LAT_IN = 5
LAT_OUT = 8
INTERPRET = False
VMEM_BYTES = 24 * 1024 * 1024


def halves(value):
    high = value.astype(BF16)
    return high, (value - high.astype(F32)).astype(BF16)


def dot3(left, right, dims):
    (lh, ll), (rh, rl) = left, right
    dot = functools.partial(lax.dot_general, dimension_numbers=dims, preferred_element_type=F32)
    return dot(lh, rh) + (dot(lh, rl) + dot(ll, rh))


def pick(pair, rows):
    return pair[0][rows], pair[1][rows]


def call(kernel, outs, name, scratch=(), smem=(), flops=0):
    def run(*args):
        moved = sum(math.prod(a.shape) for a in args) + sum(math.prod(o) for o in outs)
        return pl.pallas_call(
            kernel,
            out_shape=[jax.ShapeDtypeStruct(o, F32) for o in outs],
            in_specs=[
                pl.BlockSpec(memory_space=pltpu.SMEM if i in smem else pltpu.VMEM)
                for i in range(len(args))
            ],
            out_specs=[pl.BlockSpec(memory_space=pltpu.VMEM) for _ in outs],
            scratch_shapes=[pltpu.VMEM(shape, F32) for shape in scratch],
            compiler_params=pltpu.CompilerParams(vmem_limit_bytes=VMEM_BYTES),
            cost_estimate=pl.CostEstimate(
                flops=flops, bytes_accessed=4 * moved, transcendentals=0
            ),
            name=name,
            interpret=INTERPRET,
        )(*args)

    return run


def normed(rows):
    centred = rows - jnp.mean(rows, axis=1, keepdims=True)
    inv = 1.0 / jnp.sqrt(jnp.mean(centred * centred, axis=1, keepdims=True) + EPS)
    return centred * inv, inv


def norm_back(upstream, unit, inv):
    return inv * (
        upstream
        - jnp.mean(upstream, axis=1, keepdims=True)
        - unit * jnp.mean(upstream * unit, axis=1, keepdims=True)
    )


def project_kernel(
    patches, latents, wrl, wvl, wrt, wvt, cells, table, place,
    tn_o, tno_o, tio_o, ln_o, lno_o, lio_o, q_o, lv_o, k_o, v_o, s_o,
    tinv_s, linv_s,
):
    cell = cells[...]
    terms = []
    rest = table[...]
    for _ in range(3):
        terms.append(rest.astype(BF16))
        rest = rest - terms[-1].astype(F32)
    code = []
    for coord in (cell // (GRID * GRID), cell // GRID % GRID, cell % GRID):
        hot = lax.broadcasted_iota(jnp.int32, (GRID, cell.shape[1]), 0) == coord
        hot = jnp.where(hot, 1.0, 0.0).astype(F32).T.astype(BF16)
        dot = functools.partial(
            lax.dot_general, hot, dimension_numbers=NN, preferred_element_type=F32
        )
        code.append(dot(terms[0]) + (dot(terms[1]) + dot(terms[2])))
    tn, tinv_s[...] = normed(patches[...] + jnp.concatenate(code, axis=1))
    tn_o[...] = tn
    rows = tno_o.shape[0]
    mine = pl.ds(pl.multiple_of(place[4] * rows, 8), rows)
    tno_o[...] = tn_o[mine, :]
    tio_o[...] = tinv_s[mine, :]
    tn = halves(tn)
    k = dot3(halves(wrt[...]), tn, NT)
    k_o[...] = k
    v_o[...] = dot3(halves(wvt[...]), tn, NT)
    ln, linv_s[...] = normed(latents[...])
    ln_o[...] = ln
    mine = pl.ds(pl.multiple_of(place[5] * 8, 8), 8)
    lno_o[...] = ln_o[mine, :]
    lio_o[...] = linv_s[mine, :]
    ln = halves(ln)
    q = dot3(halves(wrl[...]), ln, NT) * (1.0 / math.sqrt(HEAD))
    q_o[...] = q
    lv_o[...] = dot3(halves(wvl[...]), ln, NT)
    q = halves(q)
    for h in range(k.shape[0] // HEAD):
        rows = slice(h * HEAD, (h + 1) * HEAD)
        s_o[h] = dot3(halves(k[rows].T), pick(q, rows), NN)


def latent_kernel(place, s, v, wol, *refs):
    pieces, (gl_o, do_o, dp_o, att_o, st_o) = refs[:-5], refs[-5:]
    shares = len(pieces) // 2
    size = pieces[0].shape[0]
    for j in range(2):
        for d in range(shares):
            share = (place[4] + shares - d) % shares
            at = share * (2 * size) + (place[3] ^ j) * size
            gl_o[pl.ds(pl.multiple_of(at, 8), size), :] = pieces[j * shares + d][...]
    heads = s.shape[0]
    do = dot3(halves(wol[...]), halves(gl_o[...]), NN)
    do_o[...] = do
    do = halves(do)
    rows_of = []
    for h in range(heads):
        rows = slice(h * HEAD, (h + 1) * HEAD)
        sh = s[h]
        top = jnp.max(sh, axis=0, keepdims=True)
        e = jnp.exp(sh - top)
        vh = v[rows, :]
        dp = dot3(halves(vh.T), pick(do, rows), NN)
        dp_o[h] = dp
        sums = jnp.sum(e, axis=0, keepdims=True), jnp.sum(e * dp, axis=0, keepdims=True)
        rows_of.append((top, *sums))
        att_o[rows, :] = dot3(halves(vh), halves(e), NN)
    stats = jnp.concatenate([r[i] for i in range(3) for r in rows_of], axis=0)
    for l in range(stats.shape[1] // 128):
        at = l * 3 * heads
        st_o[at : at + 3 * heads, :] = stats[:, l * 128 : (l + 1) * 128]


def merge_kernel(heads, *refs):
    parts, out = refs[:-1], refs[-1]
    for at in range(0, out.shape[0], 3 * heads):
        top = functools.reduce(jnp.maximum, [p[at : at + heads, :] for p in parts])
        total = sums = 0.0
        for p in parts:
            scale = jnp.exp(p[at : at + heads, :] - top)
            total = total + p[at + heads : at + 2 * heads, :] * scale
            sums = sums + p[at + 2 * heads : at + 3 * heads, :] * scale
        out[at : at + 3 * heads, :] = jnp.concatenate([top, total, sums], axis=0)


def stat_row(stats, heads, row):
    at = range(row, stats.shape[0], 3 * heads)
    return jnp.concatenate([stats[i : i + 1, :] for i in at], axis=1)


def token_kernel(s, lv, gt, wot, ds_o, dvl_o, got_o):
    gts = halves(gt[...])
    do = dot3(halves(wot[...]), gts, NT)
    lvs = halves(lv[...])
    att = []
    for h in range(s.shape[0]):
        rows = slice(h * HEAD, (h + 1) * HEAD)
        sh = s[h]
        e = jnp.exp(sh - jnp.max(sh, axis=1, keepdims=True))
        p = e * (1.0 / jnp.sum(e, axis=1, keepdims=True))
        ps = halves(p)
        lvh = pick(lvs, rows)
        att.append(dot3(lvh, ps, NT))
        doh = do[rows]
        dp = dot3(halves(doh.T), lvh, NN)
        ds_o[h] = p * (dp - jnp.sum(p * dp, axis=1, keepdims=True))
        dvl_o[rows, :] = dot3(halves(doh), ps, NN)
    got_o[...] = dot3(halves(jnp.concatenate(att, axis=0)), gts, NN)


SEND_KEEP = (((1, 2), (0, 3)), ((3, 2), (0, 1)))


def backward_kernel(
    place, s, dp, dst, local, whole, q, k, do, att, tn, dvl, got, *refs
):
    both_o, pack_o, pack_s = refs[0], refs[1:-1], refs[-1]
    heads = s.shape[0]
    chunks, slots = pack_s.shape[:2]
    wslots = slots - LAT_IN
    qs, ks, dos = halves(q[...]), halves(k[...]), halves(do[...])
    drt, dvt, drl, lat = [], [], [], []
    for h in range(heads):
        rows = slice(h * HEAD, (h + 1) * HEAD)
        top = stat_row(whole, heads, h)
        inv = 1.0 / stat_row(whole, heads, heads + h)
        delta = stat_row(whole, heads, 2 * heads + h) * inv
        p = jnp.exp(s[h] - top) * inv
        ds = halves(p * (dp[h] - delta) + dst[h])
        drt.append(dot3(pick(qs, rows), ds, NT))
        dvt.append(dot3(pick(dos, rows), halves(p), NT))
        drl.append(dot3(pick(ks, rows), ds, NN) * (1.0 / math.sqrt(HEAD)))
        lat.append(att[rows, :] * (jnp.exp(stat_row(local, heads, h) - top) * inv))
    width = drl[0].shape[1]
    rows = jnp.concatenate(
        drl + [dvl[...]] + lat + [jnp.zeros((HEAD, width), F32)], axis=0
    )
    for t in range(LAT_IN):
        pack_s[:, wslots + t] = rows[t * 128 : (t + 1) * 128].T.reshape(chunks, 8, 128)
    both = jnp.concatenate(drt + dvt, axis=0)
    both_o[...] = both
    grads = dot3(halves(both), halves(tn[...]), NN)
    index = 0
    for part in (grads, got[...]):
        for r in range(part.shape[0] // 8):
            for l in range(part.shape[1] // 128):
                pack_s[index // wslots, index % wslots] = part[
                    r * 8 : (r + 1) * 8, l * 128 : (l + 1) * 128
                ]
                index += 1
    for index in range(index, chunks * wslots):
        pack_s[index // wslots, index % wslots] = jnp.zeros((8, 128), F32)
    us = pack_o[0].shape[1]
    for j in range(2):
        for half in range(2):
            for kind in range(2):
                out = pack_o[(1 - j) * 4 + half * 2 + kind]
                for i, flip in enumerate(SEND_KEEP[half][kind]):
                    for d in range(us):
                        u = (place[0] + d) % us
                        out[i, d] = pack_s[
                            chunk_at(u, place[1] ^ half, place[2] ^ flip, place[3] ^ j)
                        ]


def rows_back_kernel(place, both, wrt, wvt, *refs):
    dtn_o, dtn_s = refs[:-1], refs[-1]
    w = halves(jnp.concatenate([wrt[...], wvt[...]], axis=0))
    dtn_s[...] = dot3(halves(both[...].T), w, NN)
    size = dtn_o[0].shape[0]
    for d, out in enumerate(dtn_o):
        at = (place[4] + d) % len(dtn_o) * size
        out[...] = dtn_s[pl.ds(pl.multiple_of(at, 8), size), :]


def chunk_at(u, w, y, c):
    return ((u * 2 + w) * 4 + y) * 2 + c


def own_rows_kernel(unit, inv, *refs):
    total = refs[0][...]
    for p in refs[1:-1]:
        total = total + p[...]
    refs[-1][...] = norm_back(total, unit[...], inv[...])


def join_rows_kernel(place, *refs):
    parts, out = refs[:-1], refs[-1]
    size = parts[0].shape[0]
    for d, p in enumerate(parts):
        at = (place[4] + len(parts) - d) % len(parts) * size
        out[pl.ds(pl.multiple_of(at, 8), size), :] = p[...]


def join_kernel(*refs):
    for i, p in enumerate(refs[:-1]):
        refs[-1][i] = p[0]


def columns(value, share, width):
    own = value[:, :width]
    for i in range(1, value.shape[1] // width):
        own = jnp.where(share == i, value[:, i * width : (i + 1) * width], own)
    return own


def rows_kernel(place, ln, wrl, wvl, wol, *refs):
    shares = wrl.shape[1] // wrl.shape[0]
    parts, chunk, outs = refs[: -shares - 1], refs[-shares - 1], refs[-shares:]
    total = parts[0][0]
    for p in parts[1:]:
        total = total + p[0]
    chunk[0] = total
    wslots = chunk.shape[1] - LAT_IN
    width, full = wrl.shape
    lat = halves(jnp.concatenate([total[wslots + t] for t in range(LAT_IN)], axis=1))
    dref, dval, att = [
        tuple(p[:, i * width : (i + 1) * width] for p in lat) for i in range(3)
    ]
    grad = dot3(dref, halves(wrl[...]), NN) + dot3(dval, halves(wvl[...]), NN)
    result = dot3(att, halves(wol[...]), NN)
    lane = lax.broadcasted_iota(jnp.int32, (8, 128), 1)
    sums = jnp.where(
        lane == 0,
        jnp.sum(grad, axis=1, keepdims=True),
        jnp.where(lane == 1, jnp.sum(grad * ln[...], axis=1, keepdims=True), 0.0),
    )
    for d, out in enumerate(outs):
        share = (place[4] + d) % shares
        out[...] = jnp.concatenate(
            [columns(grad, share, width), columns(result, share, width), sums], axis=1
        )


def finish_kernel(place, chunk, ln, linv, *refs):
    parts, out = refs[:-1], refs[-1]
    wslots = chunk.shape[1] - LAT_IN
    total = parts[0][...]
    for p in parts[1:]:
        total = total + p[...]
    full = ln.shape[1]
    width = full // len(parts)
    mean = total[:, 2 * width : 2 * width + 1] * (1.0 / full)
    along = total[:, 2 * width + 1 : 2 * width + 2] * (1.0 / full)
    own_grad = linv[...] * (
        total[:, :width] - mean - columns(ln[...], place[4], width) * along
    )
    own_out = total[:, width : 2 * width]
    lat = jnp.concatenate([chunk[0, wslots + t] for t in range(LAT_IN)], axis=1)
    lat = jnp.concatenate(
        [lat[:, : 3 * width], own_grad, own_out, jnp.zeros((8, LAT_OUT * 128 - 5 * width), F32)],
        axis=1,
    )
    for t in range(wslots):
        out[0, t] = chunk[0, t]
    for t in range(LAT_OUT):
        out[0, wslots + t] = lat[:, t * 128 : (t + 1) * 128]


def unpack_kernel(place, ln, gl, *refs):
    parts, outs, pack = refs[:16], refs[16:-1], refs[-1]
    grl_o, gvl_o, gol_o, grt_o, gvt_o, got_o, lg_o, lo_o = outs
    us = parts[0].shape[0]
    for j in range(2):
        for half in range(2):
            for flip in range(4):
                part = parts[j * 8 + half * 4 + flip]
                for d in range(us):
                    u = (place[0] + us - d) % us
                    pack[chunk_at(u, place[1] ^ half, place[2] ^ flip, place[3] ^ j)] = part[d]
    chunks, slots = pack.shape[:2]
    wslots = slots - LAT_OUT
    width = grl_o.shape[0]
    rows = jnp.concatenate(
        [pack[:, wslots + t].reshape(chunks * 8, 128).T for t in range(LAT_OUT)], axis=0
    )
    lns = halves(ln[...])
    grl_o[...] = dot3(halves(rows[:width]), lns, NN)
    gvl_o[...] = dot3(halves(rows[width : 2 * width]), lns, NN)
    gol_o[...] = dot3(halves(rows[2 * width : 3 * width]), halves(gl[...]), NT)
    lg_o[...] = rows[3 * width : 4 * width]
    lo_o[...] = rows[4 * width : 5 * width]
    index = 0
    for part in (grt_o, gvt_o, got_o):
        for r in range(part.shape[0] // 8):
            for l in range(part.shape[1] // 128):
                part[r * 8 : (r + 1) * 8, l * 128 : (l + 1) * 128] = pack[
                    index // wslots, index % wslots
                ]
                index += 1


def code_table(width):
    count = width // 6
    frequency = jnp.exp(jnp.arange(count, dtype=F32) * (-math.log(10000.0) / count))
    angles = jnp.arange(GRID, dtype=F32)[:, None] * frequency[None, :]
    return jnp.concatenate([jnp.sin(angles), jnp.cos(angles)], axis=1)


def shift(value, axis, by):
    n = lax.axis_size(axis)
    return lax.ppermute(value, axis, [(i, (i + by) % n) for i in range(n)])


def shifts(value, axis):
    return [shift(value, axis, by) for by in range(1, lax.axis_size(axis))]


def swap(value, axis, flip=1):
    return lax.ppermute(value, axis, [(i, i ^ flip) for i in range(lax.axis_size(axis))])


def body(
    patches,
    patch_index,
    latents,
    w_ref_lat,
    w_val_lat,
    w_out_lat,
    w_ref_tok,
    w_val_tok,
    w_out_tok,
    grad_tok,
    grad_lat,
):
    tokens, full = patches.shape
    lats = latents.shape[0]
    width = w_ref_lat.shape[1]
    heads = width // HEAD
    u, w, y, c, x = (lax.axis_index(a) for a in (*SLAB, "x"))
    us, xs = lax.axis_size("u"), lax.axis_size("x")
    chunks = us * 16
    assert lats == 8 * chunks
    wslots = -(-3 * (width // 8) * (full // 128) // chunks)
    wrl, wvl, wrt, wvt = w_ref_lat.T, w_val_lat.T, w_ref_tok.T, w_val_tok.T
    place = jnp.stack([u, w, y, c, x, chunk_at(u, w, y, c)]).astype(jnp.int32)

    half = width // 2
    part = lax.dynamic_slice_in_dim(grad_lat.T, c * half, half, 0)
    mine = shifts(part, "x")

    square = (heads, tokens, lats)
    stats = (3 * heads * (lats // 128), 128)
    rows = tokens // xs
    tn, tn_own, tinv, ln, ln_own, linv, q, lv, k, v, s = call(
        project_kernel,
        [
            (tokens, full),
            (rows, full),
            (rows, 1),
            (lats, full),
            (8, full),
            (8, 1),
            (width, lats),
            (width, lats),
            (width, tokens),
            (width, tokens),
            square,
        ],
        "project",
        scratch=[(tokens, 1), (lats, 1)],
        smem=(8,),
        flops=6 * width * full * (2 * tokens + 2 * lats),
    )(
        patches,
        latents,
        wrl,
        wvl,
        wrt,
        wvt,
        patch_index.reshape(1, tokens),
        code_table(full),
        place,
    )
    *mine, s = lax.optimization_barrier((*mine, s))
    mine = [part] + mine
    pieces = mine + [swap(p, "c") for p in mine]
    gl, do, dp, att, local = call(
        latent_kernel,
        [(full, lats), (width, lats), square, (width, lats), stats],
        "latent",
        smem=(0,),
        flops=6 * width * lats * (full + 2 * tokens),
    )(place, s, v, w_out_lat, *pieces)

    def merge(parts):
        return call(functools.partial(merge_kernel, heads), [stats], "merge")(*parts)[0]

    whole = merge([local, swap(local, "c")])
    whole = merge([whole] + shifts(whole, "y"))
    whole = merge([whole, swap(whole, "w")])
    whole = merge([whole] + shifts(whole, "u"))
    dst, dvl, got = call(
        token_kernel,
        [square, (width, lats), (width, full)],
        "token",
        flops=6 * width * tokens * (2 * full + 3 * lats),
    )(s, lv, grad_tok, w_out_tok)
    both, *packs = call(
        backward_kernel,
        [(2 * width, tokens)] + [(2, us, wslots + LAT_IN, 8, 128)] * 8,
        "backward",
        scratch=[(chunks, wslots + LAT_IN, 8, 128)],
        smem=(0,),
        flops=6 * width * tokens * (2 * full + 3 * lats),
    )(place, s, dp, dst, local, whole, q, k, do, att, tn, dvl, got)
    dtn = call(
        rows_back_kernel,
        [(rows, full)] * xs,
        "rows_back",
        scratch=[(tokens, full)],
        smem=(0,),
        flops=12 * width * tokens * full,
    )(place, both, wrt, wvt)

    moved = [swap(p, "c") for p in (packs[0], packs[1], packs[2], packs[3])]
    send_a, keep_a, send_b, keep_b = [
        [a[i] + b[i] for i in range(2)] for a, b in zip(packs[4:], moved)
    ]
    late_a, late_b = swap(send_a[1], "y", 1), swap(send_b[1], "y", 3)
    got_a, got_b = swap(send_a[0], "y", 1), swap(send_b[0], "y", 3)
    late_a, late_b, *dtn = lax.optimization_barrier((late_a, late_b, *dtn))
    last_a, last_b = swap(keep_a[1] + late_a, "y", 3), swap(keep_b[1] + late_b, "y", 1)
    own = [dtn[0]] + [shift(d, "x", by) for by, d in enumerate(dtn[1:], 1)]
    (own,) = call(own_rows_kernel, [(rows, full)], "own_rows")(tn_own, tinv, *own)
    owns = [own] + shifts(own, "x")
    sum_a, sum_b = keep_a[0] + got_a + last_a, keep_b[0] + got_b + last_b
    sums = sum_a + swap(sum_b, "w")
    blocks = [sums[:1]] + [shift(sums[d : d + 1], "u", d) for d in range(1, us)]
    chunk, *parts = call(
        rows_kernel,
        [(1, wslots + LAT_IN, 8, 128)] + [(8, 2 * width + 128)] * xs,
        "rows",
        smem=(0,),
    )(place, ln_own, wrl, wvl, w_out_lat, *blocks)
    parts = [parts[0]] + [shift(p, "x", by) for by, p in enumerate(parts[1:], 1)]
    (chunk,) = call(finish_kernel, [(1, wslots + LAT_OUT, 8, 128)], "finish", smem=(0,))(
        place, chunk, ln_own, linv, *parts
    )
    (four,) = call(join_kernel, [(us, wslots + LAT_OUT, 8, 128)], "join")(
        chunk, *shifts(chunk, "u")
    )
    four, *owns = lax.optimization_barrier((four, *owns))
    other = swap(four, "w")
    a1, a3, b1, b3 = swap(four, "y", 1), swap(four, "y", 3), swap(other, "y", 1), swap(other, "y", 3)
    (token_grad,) = call(join_rows_kernel, [(tokens, full)], "join_rows", smem=(0,))(
        place, *owns
    )
    parts = [four, a1, swap(a3, "y", 1), a3, other, b1, swap(b1, "y", 3), b3]
    parts[2], token_grad = lax.optimization_barrier((parts[2], token_grad))
    parts += [swap(p, "c") for p in parts]
    grl, gvl, gol, grt, gvt, got, lg, lo = call(
        unpack_kernel,
        [(width, full)] * 6 + [(width, lats)] * 2,
        "unpack",
        scratch=[(chunks, wslots + LAT_OUT, 8, 128)],
        smem=(0,),
        flops=18 * width * lats * full,
    )(place, ln, gl, *parts)
    return lo.T, token_grad, lg.T, grl.T, gvl.T, gol, grt.T, gvt.T, got


def solution(mesh):
    slab, head = mesh.devices.shape
    fine = Mesh(mesh.devices.reshape(slab // 16, 2, 4, 2, head), (*SLAB, "x"))
    rows, cols, lead = P(SLAB, None), P(None, "x"), P("x", None)
    in_specs = (rows, P(SLAB), P(), cols, cols, lead, cols, cols, lead, rows, cols)
    out_specs = (cols, rows, cols, cols, cols, lead, cols, cols, lead)
    return jax.shard_map(
        body, mesh=fine, in_specs=in_specs, out_specs=out_specs, check_vma=False
    )
```

```python
import functools
import math

import jax
import jax.numpy as jnp
from jax import lax
from jax.experimental import pallas as pl
from jax.experimental.pallas import tpu as pltpu
from jax.sharding import Mesh, PartitionSpec as P

HEAD = 64
GRID = 64
EPS = 1e-05
F32 = jnp.float32
BF16 = jnp.bfloat16
NN = (((1,), (0,)), ((), ()))
NT = (((1,), (1,)), ((), ()))
SLAB = ("u", "w", "y", "c")
LAT_IN = 5
LAT_OUT = 8
INTERPRET = False
VMEM_BYTES = 24 * 1024 * 1024


def halves(value):
    high = value.astype(BF16)
    return high, (value - high.astype(F32)).astype(BF16)


def dot3(left, right, dims):
    (lh, ll), (rh, rl) = left, right
    dot = functools.partial(lax.dot_general, dimension_numbers=dims, preferred_element_type=F32)
    return dot(lh, rh) + (dot(lh, rl) + dot(ll, rh))


def pick(pair, rows):
    return pair[0][rows], pair[1][rows]


def call(kernel, outs, name, scratch=(), smem=(), flops=0):
    def run(*args):
        moved = sum(math.prod(a.shape) for a in args) + sum(math.prod(o) for o in outs)
        return pl.pallas_call(
            kernel,
            out_shape=[jax.ShapeDtypeStruct(o, F32) for o in outs],
            in_specs=[
                pl.BlockSpec(memory_space=pltpu.SMEM if i in smem else pltpu.VMEM)
                for i in range(len(args))
            ],
            out_specs=[pl.BlockSpec(memory_space=pltpu.VMEM) for _ in outs],
            scratch_shapes=[pltpu.VMEM(shape, F32) for shape in scratch],
            compiler_params=pltpu.CompilerParams(vmem_limit_bytes=VMEM_BYTES),
            cost_estimate=pl.CostEstimate(
                flops=flops, bytes_accessed=4 * moved, transcendentals=0
            ),
            name=name,
            interpret=INTERPRET,
        )(*args)

    return run


def normed(rows):
    centred = rows - jnp.mean(rows, axis=1, keepdims=True)
    inv = 1.0 / jnp.sqrt(jnp.mean(centred * centred, axis=1, keepdims=True) + EPS)
    return centred * inv, inv


def norm_back(upstream, unit, inv):
    return inv * (
        upstream
        - jnp.mean(upstream, axis=1, keepdims=True)
        - unit * jnp.mean(upstream * unit, axis=1, keepdims=True)
    )


def tokens_kernel(
    patches, wrt, wvt, cells, table, place, tn_o, tno_o, tio_o, k_o, v_o, tinv_s
):
    cell = cells[...]
    terms = []
    rest = table[...]
    for _ in range(3):
        terms.append(rest.astype(BF16))
        rest = rest - terms[-1].astype(F32)
    code = []
    for coord in (cell // (GRID * GRID), cell // GRID % GRID, cell % GRID):
        hot = lax.broadcasted_iota(jnp.int32, (GRID, cell.shape[1]), 0) == coord
        hot = jnp.where(hot, 1.0, 0.0).astype(F32).T.astype(BF16)
        dot = functools.partial(
            lax.dot_general, hot, dimension_numbers=NN, preferred_element_type=F32
        )
        code.append(dot(terms[0]) + (dot(terms[1]) + dot(terms[2])))
    tn, tinv_s[...] = normed(patches[...] + jnp.concatenate(code, axis=1))
    tn_o[...] = tn
    rows = tno_o.shape[0]
    mine = pl.ds(pl.multiple_of(place[4] * rows, 8), rows)
    tno_o[...] = tn_o[mine, :]
    tio_o[...] = tinv_s[mine, :]
    tn = halves(tn)
    k_o[...] = dot3(halves(wrt[...]), tn, NT)
    v_o[...] = dot3(halves(wvt[...]), tn, NT)


def scores_kernel(
    latents, wrl, wvl, k, place, ln_o, lno_o, lio_o, q_o, lv_o, s_o, linv_s
):
    ln, linv_s[...] = normed(latents[...])
    ln_o[...] = ln
    mine = pl.ds(pl.multiple_of(place[5] * 8, 8), 8)
    lno_o[...] = ln_o[mine, :]
    lio_o[...] = linv_s[mine, :]
    ln = halves(ln)
    q = dot3(halves(wrl[...]), ln, NT) * (1.0 / math.sqrt(HEAD))
    q_o[...] = q
    lv_o[...] = dot3(halves(wvl[...]), ln, NT)
    q = halves(q)
    for h in range(k.shape[0] // HEAD):
        rows = slice(h * HEAD, (h + 1) * HEAD)
        s_o[h] = dot3(halves(k[rows, :].T), pick(q, rows), NN)


def latent_kernel(place, s, v, wol, *refs):
    pieces, (gl_o, do_o, dp_o, att_o, st_o) = refs[:-5], refs[-5:]
    shares = len(pieces) // 2
    size = pieces[0].shape[0]
    for j in range(2):
        for d in range(shares):
            share = (place[4] + shares - d) % shares
            at = share * (2 * size) + (place[3] ^ j) * size
            gl_o[pl.ds(pl.multiple_of(at, 8), size), :] = pieces[j * shares + d][...]
    heads = s.shape[0]
    do = dot3(halves(wol[...]), halves(gl_o[...]), NN)
    do_o[...] = do
    do = halves(do)
    rows_of = []
    for h in range(heads):
        rows = slice(h * HEAD, (h + 1) * HEAD)
        sh = s[h]
        top = jnp.max(sh, axis=0, keepdims=True)
        e = jnp.exp(sh - top)
        vh = v[rows, :]
        dp = dot3(halves(vh.T), pick(do, rows), NN)
        dp_o[h] = dp
        sums = jnp.sum(e, axis=0, keepdims=True), jnp.sum(e * dp, axis=0, keepdims=True)
        rows_of.append((top, *sums))
        att_o[rows, :] = dot3(halves(vh), halves(e), NN)
    stats = jnp.concatenate([r[i] for i in range(3) for r in rows_of], axis=0)
    for l in range(stats.shape[1] // 128):
        at = l * 3 * heads
        st_o[at : at + 3 * heads, :] = stats[:, l * 128 : (l + 1) * 128]


def merge_kernel(heads, *refs):
    parts, out = refs[:-1], refs[-1]
    for at in range(0, out.shape[0], 3 * heads):
        top = functools.reduce(jnp.maximum, [p[at : at + heads, :] for p in parts])
        total = sums = 0.0
        for p in parts:
            scale = jnp.exp(p[at : at + heads, :] - top)
            total = total + p[at + heads : at + 2 * heads, :] * scale
            sums = sums + p[at + 2 * heads : at + 3 * heads, :] * scale
        out[at : at + 3 * heads, :] = jnp.concatenate([top, total, sums], axis=0)


def stat_row(stats, heads, row):
    at = range(row, stats.shape[0], 3 * heads)
    return jnp.concatenate([stats[i : i + 1, :] for i in at], axis=1)


def token_kernel(s, lv, gt, wot, ds_o, dvl_o, got_o):
    gts = halves(gt[...])
    do = dot3(halves(wot[...]), gts, NT)
    lvs = halves(lv[...])
    att = []
    for h in range(s.shape[0]):
        rows = slice(h * HEAD, (h + 1) * HEAD)
        sh = s[h]
        e = jnp.exp(sh - jnp.max(sh, axis=1, keepdims=True))
        p = e * (1.0 / jnp.sum(e, axis=1, keepdims=True))
        ps = halves(p)
        lvh = pick(lvs, rows)
        att.append(dot3(lvh, ps, NT))
        doh = do[rows]
        dp = dot3(halves(doh.T), lvh, NN)
        ds_o[h] = p * (dp - jnp.sum(p * dp, axis=1, keepdims=True))
        dvl_o[rows, :] = dot3(halves(doh), ps, NN)
    got_o[...] = dot3(halves(jnp.concatenate(att, axis=0)), gts, NN)


SEND_KEEP = (((1, 2), (0, 3)), ((3, 2), (0, 1)))


def backward_kernel(
    place, s, dp, dst, local, whole, q, k, do, att, tn, dvl, got, *refs
):
    both_o, pack_o, pack_s = refs[0], refs[1:-1], refs[-1]
    heads = s.shape[0]
    chunks, slots = pack_s.shape[:2]
    wslots = slots - LAT_IN
    qs, ks, dos = halves(q[...]), halves(k[...]), halves(do[...])
    drt, dvt, drl, lat = [], [], [], []
    for h in range(heads):
        rows = slice(h * HEAD, (h + 1) * HEAD)
        top = stat_row(whole, heads, h)
        inv = 1.0 / stat_row(whole, heads, heads + h)
        delta = stat_row(whole, heads, 2 * heads + h) * inv
        p = jnp.exp(s[h] - top) * inv
        ds = halves(p * (dp[h] - delta) + dst[h])
        drt.append(dot3(pick(qs, rows), ds, NT))
        dvt.append(dot3(pick(dos, rows), halves(p), NT))
        drl.append(dot3(pick(ks, rows), ds, NN) * (1.0 / math.sqrt(HEAD)))
        lat.append(att[rows, :] * (jnp.exp(stat_row(local, heads, h) - top) * inv))
    width = drl[0].shape[1]
    rows = jnp.concatenate(
        drl + [dvl[...]] + lat + [jnp.zeros((HEAD, width), F32)], axis=0
    )
    for t in range(LAT_IN):
        pack_s[:, wslots + t] = rows[t * 128 : (t + 1) * 128].T.reshape(chunks, 8, 128)
    both = jnp.concatenate(drt + dvt, axis=0)
    both_o[...] = both
    grads = dot3(halves(both), halves(tn[...]), NN)
    index = 0
    for part in (grads, got[...]):
        for r in range(part.shape[0] // 8):
            for l in range(part.shape[1] // 128):
                pack_s[index // wslots, index % wslots] = part[
                    r * 8 : (r + 1) * 8, l * 128 : (l + 1) * 128
                ]
                index += 1
    for index in range(index, chunks * wslots):
        pack_s[index // wslots, index % wslots] = jnp.zeros((8, 128), F32)
    us = pack_o[0].shape[1]
    for j in range(2):
        for half in range(2):
            for kind in range(2):
                out = pack_o[(1 - j) * 4 + half * 2 + kind]
                for i, flip in enumerate(SEND_KEEP[half][kind]):
                    for d in range(us):
                        u = (place[0] + d) % us
                        out[i, d] = pack_s[
                            chunk_at(u, place[1] ^ half, place[2] ^ flip, place[3] ^ j)
                        ]


def rows_back_kernel(place, both, wrt, wvt, *refs):
    dtn_o, dtn_s = refs[:-1], refs[-1]
    w = halves(jnp.concatenate([wrt[...], wvt[...]], axis=0))
    dtn_s[...] = dot3(halves(both[...].T), w, NN)
    size = dtn_o[0].shape[0]
    for d, out in enumerate(dtn_o):
        at = (place[4] + d) % len(dtn_o) * size
        out[...] = dtn_s[pl.ds(pl.multiple_of(at, 8), size), :]


def chunk_at(u, w, y, c):
    return ((u * 2 + w) * 4 + y) * 2 + c


def own_rows_kernel(unit, inv, *refs):
    total = refs[0][...]
    for p in refs[1:-1]:
        total = total + p[...]
    refs[-1][...] = norm_back(total, unit[...], inv[...])


def join_rows_kernel(place, *refs):
    parts, out = refs[:-1], refs[-1]
    size = parts[0].shape[0]
    for d, p in enumerate(parts):
        at = (place[4] + len(parts) - d) % len(parts) * size
        out[pl.ds(pl.multiple_of(at, 8), size), :] = p[...]


def join_kernel(*refs):
    for i, p in enumerate(refs[:-1]):
        refs[-1][i] = p[0]


def columns(value, share, width):
    own = value[:, :width]
    for i in range(1, value.shape[1] // width):
        own = jnp.where(share == i, value[:, i * width : (i + 1) * width], own)
    return own


def rows_kernel(place, ln, wrl, wvl, wol, *refs):
    parts, (chunk, send, keep) = refs[:-3], refs[-3:]
    total = parts[0][0]
    for p in parts[1:]:
        total = total + p[0]
    chunk[0] = total
    wslots = chunk.shape[1] - LAT_IN
    width, full = wrl.shape
    lat = halves(jnp.concatenate([total[wslots + t] for t in range(LAT_IN)], axis=1))
    dref, dval, att = [
        tuple(p[:, i * width : (i + 1) * width] for p in lat) for i in range(3)
    ]
    grad = dot3(dref, halves(wrl[...]), NN) + dot3(dval, halves(wvl[...]), NN)
    result = dot3(att, halves(wol[...]), NN)
    lane = lax.broadcasted_iota(jnp.int32, (8, 128), 1)
    sums = jnp.where(
        lane == 0,
        jnp.sum(grad, axis=1, keepdims=True),
        jnp.where(lane == 1, jnp.sum(grad * ln[...], axis=1, keepdims=True), 0.0),
    )
    for out, flips in ((send, (3, 2)), (keep, (0, 1))):
        for i, flip in enumerate(flips):
            share = place[4] ^ flip
            out[i] = jnp.concatenate(
                [columns(grad, share, width), columns(result, share, width), sums], axis=1
            )


def finish_kernel(place, chunk, ln, linv, *refs):
    parts, out = refs[:-1], refs[-1]
    wslots = chunk.shape[1] - LAT_IN
    total = parts[0][...]
    for p in parts[1:]:
        total = total + p[...]
    full = ln.shape[1]
    width = (total.shape[1] - 128) // 2
    mean = total[:, 2 * width : 2 * width + 1] * (1.0 / full)
    along = total[:, 2 * width + 1 : 2 * width + 2] * (1.0 / full)
    own_grad = linv[...] * (
        total[:, :width] - mean - columns(ln[...], place[4], width) * along
    )
    own_out = total[:, width : 2 * width]
    lat = jnp.concatenate([chunk[0, wslots + t] for t in range(LAT_IN)], axis=1)
    lat = jnp.concatenate(
        [lat[:, : 3 * width], own_grad, own_out, jnp.zeros((8, LAT_OUT * 128 - 5 * width), F32)],
        axis=1,
    )
    for t in range(wslots):
        out[0, t] = chunk[0, t]
    for t in range(LAT_OUT):
        out[0, wslots + t] = lat[:, t * 128 : (t + 1) * 128]


def unpack_kernel(place, ln, gl, *refs):
    parts, outs, pack = refs[:16], refs[16:-1], refs[-1]
    grl_o, gvl_o, gol_o, grt_o, gvt_o, got_o, lg_o, lo_o = outs
    us = parts[0].shape[0]
    for j in range(2):
        for half in range(2):
            for flip in range(4):
                part = parts[j * 8 + half * 4 + flip]
                for d in range(us):
                    u = (place[0] + us - d) % us
                    pack[chunk_at(u, place[1] ^ half, place[2] ^ flip, place[3] ^ j)] = part[d]
    chunks, slots = pack.shape[:2]
    wslots = slots - LAT_OUT
    width = grl_o.shape[0]
    rows = jnp.concatenate(
        [pack[:, wslots + t].reshape(chunks * 8, 128).T for t in range(LAT_OUT)], axis=0
    )
    lns = halves(ln[...])
    grl_o[...] = dot3(halves(rows[:width]), lns, NN)
    gvl_o[...] = dot3(halves(rows[width : 2 * width]), lns, NN)
    gol_o[...] = dot3(halves(rows[2 * width : 3 * width]), halves(gl[...]), NT)
    lg_o[...] = rows[3 * width : 4 * width]
    lo_o[...] = rows[4 * width : 5 * width]
    index = 0
    for part in (grt_o, gvt_o, got_o):
        for r in range(part.shape[0] // 8):
            for l in range(part.shape[1] // 128):
                part[r * 8 : (r + 1) * 8, l * 128 : (l + 1) * 128] = pack[
                    index // wslots, index % wslots
                ]
                index += 1


def code_table(width):
    count = width // 6
    frequency = jnp.exp(jnp.arange(count, dtype=F32) * (-math.log(10000.0) / count))
    angles = jnp.arange(GRID, dtype=F32)[:, None] * frequency[None, :]
    return jnp.concatenate([jnp.sin(angles), jnp.cos(angles)], axis=1)


def shift(value, axis, by):
    n = lax.axis_size(axis)
    return lax.ppermute(value, axis, [(i, (i + by) % n) for i in range(n)])


def shifts(value, axis):
    return [shift(value, axis, by) for by in range(1, lax.axis_size(axis))]


def swap(value, axis, flip=1):
    return lax.ppermute(value, axis, [(i, i ^ flip) for i in range(lax.axis_size(axis))])


def body(
    patches,
    patch_index,
    latents,
    w_ref_lat,
    w_val_lat,
    w_out_lat,
    w_ref_tok,
    w_val_tok,
    w_out_tok,
    grad_tok,
    grad_lat,
):
    tokens, full = patches.shape
    lats = latents.shape[0]
    width = w_ref_lat.shape[1]
    heads = width // HEAD
    u, w, y, c, x = (lax.axis_index(a) for a in (*SLAB, "x"))
    us, xs = lax.axis_size("u"), lax.axis_size("x")
    chunks = us * 16
    assert lats == 8 * chunks
    wslots = -(-3 * (width // 8) * (full // 128) // chunks)
    wrl, wvl, wrt, wvt = w_ref_lat.T, w_val_lat.T, w_ref_tok.T, w_val_tok.T
    place = jnp.stack([u, w, y, c, x, chunk_at(u, w, y, c)]).astype(jnp.int32)

    half = width // 2
    part = lax.dynamic_slice_in_dim(grad_lat.T, c * half, half, 0)
    mine = shifts(part, "x")

    square = (heads, tokens, lats)
    stats = (3 * heads * (lats // 128), 128)
    rows = tokens // xs
    tn, tn_own, tinv, k, v = call(
        tokens_kernel,
        [(tokens, full), (rows, full), (rows, 1), (width, tokens), (width, tokens)],
        "tokens",
        scratch=[(tokens, 1)],
        smem=(5,),
        flops=12 * width * full * tokens,
    )(patches, wrt, wvt, patch_index.reshape(1, tokens), code_table(full), place)
    ln, ln_own, linv, q, lv, s = call(
        scores_kernel,
        [(lats, full), (8, full), (8, 1), (width, lats), (width, lats), square],
        "scores",
        scratch=[(lats, 1)],
        smem=(4,),
        flops=12 * width * full * lats,
    )(latents, wrl, wvl, k, place)
    *mine, s = lax.optimization_barrier((*mine, s))
    mine = [part] + mine
    pieces = mine + [swap(p, "c") for p in mine]
    gl, do, dp, att, local = call(
        latent_kernel,
        [(full, lats), (width, lats), square, (width, lats), stats],
        "latent",
        smem=(0,),
        flops=6 * width * lats * (full + 2 * tokens),
    )(place, s, v, w_out_lat, *pieces)

    def merge(parts):
        return call(functools.partial(merge_kernel, heads), [stats], "merge")(*parts)[0]

    whole = merge([local, swap(local, "c")])
    whole = merge([whole] + shifts(whole, "y"))
    whole = merge([whole, swap(whole, "w")])
    whole = merge([whole] + shifts(whole, "u"))
    dst, dvl, got = call(
        token_kernel,
        [square, (width, lats), (width, full)],
        "token",
        flops=6 * width * tokens * (2 * full + 3 * lats),
    )(s, lv, grad_tok, w_out_tok)
    both, *packs = call(
        backward_kernel,
        [(2 * width, tokens)] + [(2, us, wslots + LAT_IN, 8, 128)] * 8,
        "backward",
        scratch=[(chunks, wslots + LAT_IN, 8, 128)],
        smem=(0,),
        flops=6 * width * tokens * (2 * full + 3 * lats),
    )(place, s, dp, dst, local, whole, q, k, do, att, tn, dvl, got)
    dtn = call(
        rows_back_kernel,
        [(rows, full)] * xs,
        "rows_back",
        scratch=[(tokens, full)],
        smem=(0,),
        flops=12 * width * tokens * full,
    )(place, both, wrt, wvt)

    moved = [swap(p, "c") for p in (packs[0], packs[1], packs[2], packs[3])]
    send_a, keep_a, send_b, keep_b = [
        [a[i] + b[i] for i in range(2)] for a, b in zip(packs[4:], moved)
    ]
    late_a, late_b = swap(send_a[1], "y", 1), swap(send_b[1], "y", 3)
    got_a, got_b = swap(send_a[0], "y", 1), swap(send_b[0], "y", 3)
    late_a, late_b, *dtn = lax.optimization_barrier((late_a, late_b, *dtn))
    last_a, last_b = swap(keep_a[1] + late_a, "y", 3), swap(keep_b[1] + late_b, "y", 1)
    own = [dtn[0]] + [shift(d, "x", by) for by, d in enumerate(dtn[1:], 1)]
    (own,) = call(own_rows_kernel, [(rows, full)], "own_rows")(tn_own, tinv, *own)
    owns = [own] + shifts(own, "x")
    sum_a, sum_b = keep_a[0] + got_a + last_a, keep_b[0] + got_b + last_b
    sums = sum_a + swap(sum_b, "w")
    blocks = [sums[:1]] + [shift(sums[d : d + 1], "u", d) for d in range(1, us)]
    chunk, send, keep = call(
        rows_kernel,
        [(1, wslots + LAT_IN, 8, 128)] + [(2, 8, 2 * width + 128)] * 2,
        "rows",
        smem=(0,),
    )(place, ln_own, wrl, wvl, w_out_lat, *blocks)
    got = swap(send, "x", 3)
    parts = [keep[0], got[0], swap(keep[1] + got[1], "x", 1)]
    (chunk,) = call(finish_kernel, [(1, wslots + LAT_OUT, 8, 128)], "finish", smem=(0,))(
        place, chunk, ln_own, linv, *parts
    )
    (four,) = call(join_kernel, [(us, wslots + LAT_OUT, 8, 128)], "join")(
        chunk, *shifts(chunk, "u")
    )
    four, *owns = lax.optimization_barrier((four, *owns))
    other = swap(four, "w")
    a1, a3, b1, b3 = swap(four, "y", 1), swap(four, "y", 3), swap(other, "y", 1), swap(other, "y", 3)
    (token_grad,) = call(join_rows_kernel, [(tokens, full)], "join_rows", smem=(0,))(
        place, *owns
    )
    parts = [four, a1, swap(a3, "y", 1), a3, other, b1, swap(b1, "y", 3), b3]
    parts[2], token_grad = lax.optimization_barrier((parts[2], token_grad))
    parts += [swap(p, "c") for p in parts]
    grl, gvl, gol, grt, gvt, got, lg, lo = call(
        unpack_kernel,
        [(width, full)] * 6 + [(width, lats)] * 2,
        "unpack",
        scratch=[(chunks, wslots + LAT_OUT, 8, 128)],
        smem=(0,),
        flops=18 * width * lats * full,
    )(place, ln, gl, *parts)
    return lo.T, token_grad, lg.T, grl.T, gvl.T, gol, grt.T, gvt.T, got


def solution(mesh):
    slab, head = mesh.devices.shape
    fine = Mesh(mesh.devices.reshape(slab // 16, 2, 4, 2, head), (*SLAB, "x"))
    rows, cols, lead = P(SLAB, None), P(None, "x"), P("x", None)
    in_specs = (rows, P(SLAB), P(), cols, cols, lead, cols, cols, lead, rows, cols)
    out_specs = (cols, rows, cols, cols, cols, lead, cols, cols, lead)
    return jax.shard_map(
        body, mesh=fine, in_specs=in_specs, out_specs=out_specs, check_vma=False
    )
```
